32 devices in a mesh: prow: 8 (over y, x, core), pcol: 4 (over z).
Axes of the slice: x: 2, y: 2, z: 4, core: 2. Of those that a mesh axis runs over, the one named last changes fastest.
Arguments:
- anc_inverse: bfloat16 [2, 2, 8, 256, 4, 4, 256], P(None, None, 'prow', None, None, 'pcol'), may hold values from -6 to 6
- factor_panel: bfloat16 [2, 2, 8, 256, 4, 4, 256], P(None, None, 'prow', None, None, 'pcol'), may hold values from -0.09375 to 0.09375
- diag_inverse: bfloat16 [2, 4, 4, 256, 2, 8, 256], P(None, None, 'pcol', None, None, 'prow'), may hold values from -6 to 6
- block_pattern: int32 [2, 16, 16], replicated, may hold values from 0 to 1, as said below
Outputs:
- sigma_off: bfloat16 [2, 2, 8, 256, 4, 4, 256], P(None, None, 'prow', None, None, 'pcol')
- sigma_diag: bfloat16 [2, 4, 4, 256, 2, 8, 256], P(None, None, 'pcol', None, None, 'prow')
The draws below stay inside these ranges and needn't reach their ends.
Inputs may be any that keep to these rules, and one draw needn't show every extreme that they name: `block_pattern`: symmetric in its last two dimensions, with ones on the diagonal.
All inputs are finite; a program needn't handle non-finite values.
Results may differ from the reference program's by a relative error of at most 0.0039.
Values may be sent and summed in bfloat16 or wider, within the bound.
A program may use at most 128 MiB of HBM per device.

```python
import jax
import jax.numpy as jnp
from jax import lax

BLK = 256
W = 4096
ANC = 4096
SN = 2
AB = 16
WB = 16
N_PROW = 8
N_PCOL = 4


def draw_block_pattern(key, part):
    key = jax.random.fold_in(key, 7)
    blocks = ANC // BLK
    raw_draw = jax.random.randint(key, (SN, blocks, blocks), 0, 16)
    row_ids = lax.broadcasted_iota(jnp.int32, (SN, blocks, blocks), 1)
    col_ids = lax.broadcasted_iota(jnp.int32, (SN, blocks, blocks), 2)
    symmetric = jnp.where(row_ids <= col_ids, raw_draw, jnp.swapaxes(raw_draw, 1, 2))
    threshold = 4 + 12 * jnp.maximum(row_ids, col_ids) // blocks
    chosen = (symmetric < threshold) | (row_ids == col_ids)
    return jnp.where(chosen, 1, 0).astype(jnp.int32)


def shard_levels(key, dims, split, smallest, top_value):
    gain = 1.0
    for axis_at, parts in split:
        draws = jax.random.uniform(jax.random.fold_in(jax.random.fold_in(key, 6), axis_at), (parts,), jnp.float32, smallest / len(split), top_value / len(split))
        gain = gain * jnp.repeat(jnp.exp(draws), dims[axis_at] // parts).reshape((-1,) + (1,) * (len(dims) - 1 - axis_at))
    return gain


def centred(own_key, shape, width, bound, cuts=(), kind=jnp.bfloat16):
    values = width * jax.random.normal(own_key, shape, jnp.float32)
    if cuts:
        values = values * shard_levels(own_key, shape, cuts, -0.22, 0.18)
    return jnp.clip(values, -bound, bound).astype(kind)


def setup_inputs(seed: int = 0) -> dict:
    seeds = jax.random.split(jax.random.key(seed), 5)
    return {
        "anc_inverse": centred(seeds[0], (SN, AB // N_PROW, N_PROW, BLK, AB // N_PCOL, N_PCOL, BLK), 1.0, 6.0, ((2, 8), (5, 4))),
        "factor_panel": centred(seeds[1], (SN, AB // N_PROW, N_PROW, BLK, WB // N_PCOL, N_PCOL, BLK), ANC ** -0.5, 0.09375, ((2, 8), (5, 4))),
        "diag_inverse": centred(seeds[2], (SN, WB // N_PCOL, N_PCOL, BLK, WB // N_PROW, N_PROW, BLK), 1.0, 6.0, ((2, 4), (5, 8))),
        "block_pattern": draw_block_pattern(jax.random.fold_in(seeds[4], 71), 0),
    }


def reference(anc_inverse, factor_panel, diag_inverse, block_pattern):
    dense_mask = jnp.repeat(jnp.repeat(block_pattern, BLK, axis=1), BLK, axis=2)
    masked_inv = anc_inverse.reshape(SN, ANC, ANC)
    masked_inv = jnp.where(dense_mask != 0, masked_inv, jnp.zeros_like(masked_inv))
    factor_rows = factor_panel.reshape(SN, ANC, W)
    given_diag = diag_inverse.reshape(SN, W, W)
    off_list = []
    diag_list = []
    for supernode in range(SN):
        product = jnp.dot(masked_inv[supernode], factor_rows[supernode], preferred_element_type=jnp.float32)
        off_block = (-product).astype(jnp.bfloat16)
        inner_sum = jnp.dot(factor_rows[supernode].T, off_block, preferred_element_type=jnp.float32)
        diag_block = (given_diag[supernode].astype(jnp.float32) - inner_sum).astype(jnp.bfloat16)
        off_list.append(off_block)
        diag_list.append(diag_block)
    sigma_off = jnp.stack(off_list).reshape(factor_panel.shape)
    sigma_diag = jnp.stack(diag_list).reshape(diag_inverse.shape)
    return sigma_off, sigma_diag
```

```python
import jax
import jax.numpy as jnp
from jax import lax
from jax.sharding import PartitionSpec as P


def invert_window(anc_local, panel_local, diag_local, owned_rows, col_index):
    nodes_here, rows_loc, _, width_blk, cols_loc, _, _ = anc_local.shape
    panel_cols = panel_local.shape[4]
    col_devices = lax.axis_size("pcol")
    row_devices = lax.axis_size("prow")
    diag_cols = diag_local.shape[4]
    own_mask = lax.dynamic_slice_in_dim(owned_rows, col_index, 1, 4)
    keep_mask = own_mask[:, :, :, None, :, :, None] != 0
    masked = jnp.where(keep_mask, anc_local, jnp.zeros_like(anc_local))
    masked_all = lax.all_gather(masked, "pcol", axis=5, tiled=True)
    panel_all = lax.all_gather(panel_local, "prow", axis=2, tiled=True)
    panel_rows = panel_all.reshape(
        nodes_here, cols_loc, col_devices, width_blk, panel_cols, width_blk
    )
    product = jnp.einsum(
        "sraicbj,scbjwm->sraiwm", masked_all, panel_rows, preferred_element_type=jnp.float32
    )
    sigma_off = (-product).astype(jnp.bfloat16)[:, :, :, :, :, None, :]
    all_cols = lax.all_gather(sigma_off, "pcol", axis=5, tiled=True)
    by_owner = all_cols.reshape(
        nodes_here, rows_loc, 1, width_blk, diag_cols, row_devices, width_blk
    )
    own_cols = lax.all_to_all(by_owner, "prow", split_axis=5, concat_axis=2, tiled=True)
    inner_sum = jnp.einsum(
        "sraiwbm,sraivnk->swbmvnk", panel_all, own_cols, preferred_element_type=jnp.float32
    )
    sigma_diag = (diag_local.astype(jnp.float32) - inner_sum).astype(jnp.bfloat16)
    return (sigma_off, sigma_diag)


def on_device(anc_inverse, factor_panel, diag_inverse, block_pattern):
    row_index = lax.axis_index("prow")
    col_index = lax.axis_index("pcol")
    row_devices = lax.axis_size("prow")
    col_devices = lax.axis_size("pcol")
    nodes_all = anc_inverse.shape[0]
    pattern_grid = block_pattern.reshape(
        nodes_all, anc_inverse.shape[1], row_devices, anc_inverse.shape[4], col_devices
    )
    owned_rows = lax.dynamic_slice_in_dim(pattern_grid, row_index, 1, 2)
    off_list = []
    diag_list = []
    for supernode in range(nodes_all):
        off_block, diag_block = invert_window(
            anc_inverse[supernode : supernode + 1],
            factor_panel[supernode : supernode + 1],
            diag_inverse[supernode : supernode + 1],
            owned_rows[supernode : supernode + 1],
            col_index,
        )
        off_list.append(off_block)
        diag_list.append(diag_block)
    return (jnp.concatenate(off_list, axis=0), jnp.concatenate(diag_list, axis=0))


def solution(mesh):
    return jax.shard_map(
        on_device,
        mesh=mesh,
        in_specs=(
            P(None, None, "prow", None, None, "pcol", None),
            P(None, None, "prow", None, None, "pcol", None),
            P(None, None, "pcol", None, None, "prow", None),
            P(),
        ),
        out_specs=(
            P(None, None, "prow", None, None, "pcol", None),
            P(None, None, "pcol", None, None, "prow", None),
        ),
        check_vma=False,
    )
```

```python
import functools

import jax
import jax.numpy as jnp
from jax import lax
from jax.experimental import pallas as pl
from jax.experimental.pallas import tpu as pltpu
from jax.sharding import PartitionSpec as P

OWN, NEAR = 0, 1
RIGHT, LEFT = 0, 1


def kernel(
    row_devices, col_devices, rows_loc, blk, cols_loc, diag_cols,
    s_in, u_in, d_in,
    o_all, d_out,
    u_buf, s_buf, o_mine, o_stage, acc,
    ring_send, ring_recv, sib_send, sib_recv, s_send, s_recv, near_send, near_recv,
    o_send, o_recv, mine_send, mine_recv, own_sem, keep_sem,
):
    nodes = s_in.shape[0]
    rows = rows_loc * blk
    chips = row_devices // 2
    half = chips // 2
    last = col_devices - 1
    p = lax.axis_index("prow")
    q = lax.axis_index("pcol")
    core = lax.rem(p, 2)
    flip = 1 - 2 * core
    inner = (q >= 1) & (q <= last - 1)
    helper = (q == 1) | (q == last - 1)
    end = (q == 0) | (q == last)
    near_q = jnp.where(q <= 1, 0, last)

    def along(n):
        high = n // half
        return n + high * (3 * half - 1 - 2 * n)

    chip = p // 2
    pos = along(chip)

    def slot(off):
        return along(lax.rem(pos + off + chips, chips)) * 2 + core

    def remote(src, dst, send, recv, to_p, to_q):
        return pltpu.make_async_remote_copy(
            src_ref=src, dst_ref=dst, send_sem=send, recv_sem=recv,
            device_id=(to_p, to_q), device_id_type=pl.DeviceIdType.MESH,
        )

    barrier = pltpu.get_barrier_semaphore()
    for step in range(1, row_devices):
        pl.semaphore_signal(
            barrier, inc=1, device_id=(lax.rem(p + step, row_devices), q),
            device_id_type=pl.DeviceIdType.MESH,
        )

    @pl.when(q > 0)
    def _():
        pl.semaphore_signal(
            barrier, inc=1, device_id=(p, q - 1), device_id_type=pl.DeviceIdType.MESH
        )

    @pl.when(q < last)
    def _():
        pl.semaphore_signal(
            barrier, inc=1, device_id=(p, q + 1), device_id_type=pl.DeviceIdType.MESH
        )

    @pl.when(inner)
    def _():
        pl.semaphore_wait(barrier, row_devices + 1)

    @pl.when(end)
    def _():
        pl.semaphore_wait(barrier, row_devices)

    def part(which, sn, at, step, way):
        if step < half:
            return u_buf.at[which, sn, at]
        cut = rows // 2
        return u_buf.at[which, sn, at, pl.ds(0 if way == RIGHT else cut, cut)]

    def ring(which, sn, way, step):
        sign = 1 if way == RIGHT else -1
        at = slot(-sign * (step - 1))
        dst = part(which, sn, at, step, way)
        src = u_in.at[sn] if (which == OWN and step == 1 and half > 1) else dst
        return remote(
            src, dst, ring_send.at[which, sn, way, step - 1],
            ring_recv.at[which, sn, way, step - 1], slot(sign), q,
        )

    def ring_wait(which, sn, way, step):
        sign = 1 if way == RIGHT else -1
        here = part(which, sn, slot(-sign * step), step, way)
        remote(
            here, here, ring_send.at[which, sn, way, step - 1],
            ring_recv.at[which, sn, way, step - 1], slot(sign), q,
        ).wait_recv()

    def sib(which, sn, off):
        at = slot(off)
        dst = u_buf.at[which, sn, at]
        src = u_in.at[sn] if (which == OWN and off == 0) else dst
        return remote(
            src, dst, sib_send.at[which, sn, off + half - 1],
            sib_recv.at[which, sn, off + half - 1], p + flip, q,
        )

    def sib_wait(which, sn, off):
        here = u_buf.at[which, sn, slot(off) + flip]
        remote(
            here, here, sib_send.at[which, sn, off + half - 1],
            sib_recv.at[which, sn, off + half - 1], p + flip, q,
        ).wait_recv()

    def ring_begin(which, sn):
        ring(which, sn, RIGHT, 1).start()
        ring(which, sn, LEFT, 1).start()
        sib(which, sn, 0).start()

    def ring_step(which, sn, step):
        for way in (RIGHT, LEFT):
            ring_wait(which, sn, way, step)
            if step < half:
                ring(which, sn, way, step + 1).start()
                sib(which, sn, -step if way == RIGHT else step).start()
        if step == half:
            sib(which, sn, half).start()

    def sib_all(which, sn):
        for off in range(1 - half, half + 1):
            sib_wait(which, sn, off)

    def ring_sent(which, sn):
        for step in range(1, half + 1):
            ring(which, sn, RIGHT, step).wait_send()
            ring(which, sn, LEFT, step).wait_send()
        for off in range(1 - half, half + 1):
            sib(which, sn, off).wait_send()

    def s_copy(sn, at, way):
        src = s_buf.at[sn, at]
        return remote(
            src, src, s_send.at[sn, at, way], s_recv.at[sn, at], p,
            q + 1 if way == RIGHT else q - 1,
        )

    def s_own(sn, way):
        return remote(
            s_in.at[sn], s_buf.at[sn, q], s_send.at[sn, q, way], s_recv.at[sn, q], p,
            q + 1 if way == RIGHT else q - 1,
        )

    up_ok = q + 1 <= last - 1
    down_ok = q - 1 >= 1

    def s_begin(sn):
        @pl.when(up_ok)
        def _():
            s_own(sn, RIGHT).start()

        @pl.when(down_ok)
        def _():
            s_own(sn, LEFT).start()

    def s_sent(sn):
        @pl.when(up_ok)
        def _():
            s_own(sn, RIGHT).wait_send()

        @pl.when(down_ok)
        def _():
            s_own(sn, LEFT).wait_send()

        for dist in range(1, col_devices):
            @pl.when((q - dist >= 0) & inner & up_ok)
            def _():
                s_copy(sn, q - dist, RIGHT).wait_send()

            @pl.when((q + dist <= last) & inner & down_ok)
            def _():
                s_copy(sn, q + dist, LEFT).wait_send()

    def s_step(sn, dist):
        for way, at, there, onward in (
            (RIGHT, q - dist, q - dist >= 0, up_ok),
            (LEFT, q + dist, q + dist <= last, down_ok),
        ):
            @pl.when(there & inner)
            def _():
                s_copy(sn, at, way).wait_recv()

                @pl.when(onward)
                def _():
                    s_copy(sn, at, way).start()

    def near(sn):
        return remote(
            u_in.at[sn], u_buf.at[NEAR, sn, p], near_send.at[sn], near_recv.at[sn], p,
            jnp.where(q == 0, 1, jnp.where(q == last, last - 1, near_q)),
        )

    def o_copy(sn, at, way, src=None):
        dst = o_all.at[sn, at]
        return remote(
            dst if src is None else src, dst, o_send.at[sn, at, way], o_recv.at[sn, at], p,
            q + 1 if way == RIGHT else q - 1,
        )

    def mine_each(sn, at, remote_do, local_do):
        for m in range(cols_loc):
            v = at + col_devices * m
            to_p = lax.rem(v, row_devices)
            k = v // row_devices
            if remote_do is not None:
                @pl.when(to_p != p)
                def _():
                    remote_do(
                        remote(
                            o_all.at[sn, at, m], o_mine.at[sn, k, p],
                            mine_send.at[sn, at, m], mine_recv.at[sn, k, p], to_p, q,
                        )
                    )

            if local_do is not None:
                @pl.when(to_p == p)
                def _():
                    local_do(
                        pltpu.make_async_copy(
                            o_all.at[sn, at, m], o_mine.at[sn, k, p], mine_recv.at[sn, k, p]
                        )
                    )

    def hand_out(sn, at):
        mine_each(sn, at, lambda c: c.start(), lambda c: c.start())

    def make_o(sn, which, at):
        for off in range(1 - half, half + 1):
            sib_wait(which, sn, off)
        acc[...] = jnp.zeros_like(acc)

        def add(src_p, carry):
            left = jnp.concatenate(
                [
                    s_buf[
                        sn, lax.rem(a * row_devices + src_p, col_devices),
                        (a * row_devices + src_p) // col_devices,
                    ]
                    for a in range(rows_loc)
                ],
                axis=1,
            )
            for m in range(cols_loc):
                acc[:rows, m * blk : (m + 1) * blk] += jnp.dot(
                    left, u_buf[which, sn, src_p, :, m * blk : (m + 1) * blk],
                    preferred_element_type=jnp.float32,
                )
            return carry

        lax.fori_loop(0, row_devices, add, 0)
        for m in range(cols_loc):
            o_stage[sn, which, m] = (-acc[:rows, m * blk : (m + 1) * blk]).astype(o_stage.dtype)
        stage = o_stage.at[sn, which]
        o_copy(sn, at, RIGHT, stage).start()
        o_copy(sn, at, LEFT, stage).start()
        keep = pltpu.make_async_copy(stage, o_all.at[sn, at], keep_sem.at[sn, which])
        keep.start()
        keep.wait()
        hand_out(sn, at)

    def o_step(sn, dist, extra):
        for way, origin, there, onward in (
            (RIGHT, q - dist, q - dist >= 1, q < last),
            (LEFT, q + dist, q + dist <= last - 1, q > 0),
        ):
            if extra:
                there = there & ((origin == 1) | (origin == last - 1))
                at = jnp.where(origin == 1, 0, last)
            else:
                at = origin
            @pl.when(there)
            def _():
                o_copy(sn, at, way).wait_recv()

                @pl.when(onward)
                def _():
                    o_copy(sn, at, way).start()

                hand_out(sn, at)

    def o_sent(sn):
        for extra in (False, True):
            if extra:
                first = helper
                at = near_q
            else:
                first = inner
                at = q
            @pl.when(first)
            def _():
                o_copy(sn, at, RIGHT).wait_send()
                o_copy(sn, at, LEFT).wait_send()
                mine_each(sn, at, lambda c: c.wait_send(), None)

            for dist in range(1, col_devices - 1):
                for way, origin, there, onward in (
                    (RIGHT, q - dist, q - dist >= 1, q < last),
                    (LEFT, q + dist, q + dist <= last - 1, q > 0),
                ):
                    if extra:
                        there = there & ((origin == 1) | (origin == last - 1))
                        at = jnp.where(origin == 1, 0, last)
                    else:
                        at = origin
                    @pl.when(there & onward)
                    def _():
                        o_copy(sn, at, way).wait_send()

                    @pl.when(there)
                    def _():
                        mine_each(sn, at, lambda c: c.wait_send(), None)

    def make_d(sn):
        acc[...] = jnp.zeros_like(acc)

        def add(src_p, carry):
            for k in range(diag_cols):
                pltpu.make_async_copy(
                    o_mine.at[sn, k, src_p], o_mine.at[sn, k, src_p], mine_recv.at[sn, k, src_p]
                ).wait()
                block = o_mine[sn, k, src_p]
                for m in range(cols_loc):
                    acc[k * blk : (k + 1) * blk, m * blk : (m + 1) * blk] += lax.dot_general(
                        block, u_buf[OWN, sn, src_p, :, m * blk : (m + 1) * blk],
                        (((0,), (0,)), ((), ())), preferred_element_type=jnp.float32,
                    )
            return carry

        lax.fori_loop(0, row_devices, add, 0)
        for k in range(diag_cols):
            for m in range(cols_loc):
                inner_sum = acc[k * blk : (k + 1) * blk, m * blk : (m + 1) * blk].T
                given = d_in[sn, m * blk : (m + 1) * blk, k * blk : (k + 1) * blk]
                d_out[sn, m * blk : (m + 1) * blk, k * blk : (k + 1) * blk] = (
                    given.astype(jnp.float32) - inner_sum
                ).astype(d_out.dtype)

    for sn in range(nodes):
        pltpu.make_async_copy(u_in.at[sn], u_buf.at[OWN, sn, p], own_sem.at[0, sn]).start()
        pltpu.make_async_copy(s_in.at[sn], s_buf.at[sn, q], own_sem.at[1, sn]).start()

    def near_begin(sn):
        @pl.when(end)
        def _():
            near(sn).start()

    s_begin(0)
    near_begin(0)
    ring_begin(OWN, 0)
    for sn in range(nodes):
        pltpu.make_async_copy(u_in.at[sn], u_buf.at[OWN, sn, p], own_sem.at[0, sn]).wait()
        pltpu.make_async_copy(s_in.at[sn], s_buf.at[sn, q], own_sem.at[1, sn]).wait()

    for sn in range(nodes):
        ring_step(OWN, sn, 1)
        s_step(sn, 1)
        if sn + 1 < nodes:
            s_begin(sn + 1)
            near_begin(sn + 1)
            ring_begin(OWN, sn + 1)

        @pl.when(helper)
        def _():
            near(sn).wait_recv()
            ring_begin(NEAR, sn)

        for step in range(2, half + 1):
            ring_step(OWN, sn, step)
        for dist in range(2, col_devices):
            s_step(sn, dist)

        if sn + 1 == nodes:
            @pl.when(helper)
            def _():
                for step in range(1, half + 1):
                    for other in range(nodes):
                        ring_step(NEAR, other, step)

        @pl.when(inner)
        def _():
            make_o(sn, OWN, q)

        @pl.when(end)
        def _():
            sib_all(OWN, sn)

    for sn in range(nodes):
        @pl.when(helper)
        def _():
            make_o(sn, NEAR, near_q)

        for dist in range(1, col_devices - 1):
            o_step(sn, dist, False)
        for dist in range(1, col_devices - 1):
            o_step(sn, dist, True)

    for sn in range(nodes):
        make_d(sn)

    for sn in range(nodes):
        ring_sent(OWN, sn)
        s_sent(sn)
        o_sent(sn)

        @pl.when(helper)
        def _():
            ring_sent(NEAR, sn)

        @pl.when(end)
        def _():
            near(sn).wait_send()


def on_device(anc_inverse, factor_panel, diag_inverse, block_pattern):
    row_index = lax.axis_index("prow")
    col_index = lax.axis_index("pcol")
    row_devices = lax.axis_size("prow")
    col_devices = lax.axis_size("pcol")
    nodes, rows_loc, _, blk, cols_loc, _, _ = anc_inverse.shape
    panel_cols = factor_panel.shape[4]
    diag_cols = diag_inverse.shape[4]
    rows = rows_loc * blk
    pattern_grid = block_pattern.reshape(nodes, rows_loc, row_devices, cols_loc, col_devices)
    owned = lax.dynamic_slice_in_dim(pattern_grid, row_index, 1, 2)
    owned = lax.dynamic_slice_in_dim(owned, col_index, 1, 4)
    masked = jnp.where(owned[:, :, :, None, :, :, None] != 0, anc_inverse, jnp.zeros_like(anc_inverse))
    s_in = masked.reshape(nodes, rows, cols_loc, blk).transpose(0, 2, 1, 3)
    u_in = factor_panel.reshape(nodes, rows, panel_cols * blk)
    d_in = diag_inverse.reshape(nodes, panel_cols * blk, diag_cols * blk)
    half = row_devices // 4
    dma = pltpu.SemaphoreType.DMA
    bf16 = jnp.bfloat16
    o_all, d_out = pl.pallas_call(
        functools.partial(
            kernel, row_devices, col_devices, rows_loc, blk, panel_cols, diag_cols
        ),
        out_shape=(
            jax.ShapeDtypeStruct((nodes, col_devices, panel_cols, rows, blk), bf16),
            jax.ShapeDtypeStruct(d_in.shape, bf16),
        ),
        in_specs=[
            pl.BlockSpec(memory_space=pl.ANY),
            pl.BlockSpec(memory_space=pl.ANY),
            pl.BlockSpec(memory_space=pltpu.VMEM),
        ],
        out_specs=(
            pl.BlockSpec(memory_space=pl.ANY),
            pl.BlockSpec(memory_space=pltpu.VMEM),
        ),
        scratch_shapes=[
            pltpu.VMEM((2, nodes, row_devices, rows, panel_cols * blk), bf16),
            pltpu.VMEM((nodes, col_devices, cols_loc, rows, blk), bf16),
            pltpu.VMEM((nodes, diag_cols, row_devices, rows, blk), bf16),
            pltpu.VMEM((nodes, 2, panel_cols, rows, blk), bf16),
            pltpu.VMEM((max(rows, diag_cols * blk), panel_cols * blk), jnp.float32),
            dma((2, nodes, 2, half)),
            dma((2, nodes, 2, half)),
            dma((2, nodes, 2 * half)),
            dma((2, nodes, 2 * half)),
            dma((nodes, col_devices, 2)),
            dma((nodes, col_devices)),
            dma((nodes,)),
            dma((nodes,)),
            dma((nodes, col_devices, 2)),
            dma((nodes, col_devices)),
            dma((nodes, col_devices, panel_cols)),
            dma((nodes, diag_cols, row_devices)),
            dma((2, nodes)),
            dma((nodes, 2)),
        ],
        compiler_params=pltpu.CompilerParams(
            collective_id=0, has_side_effects=True, vmem_limit_bytes=62 * 1024 * 1024
        ),
        cost_estimate=pl.CostEstimate(
            flops=18 * 10**9, bytes_accessed=40 * 2**20, transcendentals=0
        ),
    )(s_in, u_in, d_in)
    off = lax.dynamic_slice_in_dim(o_all, col_index, 1, 1)[:, 0]
    sigma_off = off.transpose(0, 2, 1, 3).reshape(factor_panel.shape)
    return (sigma_off, d_out.reshape(diag_inverse.shape))


def solution(mesh):
    return jax.shard_map(
        on_device,
        mesh=mesh,
        in_specs=(
            P(None, None, "prow", None, None, "pcol", None),
            P(None, None, "prow", None, None, "pcol", None),
            P(None, None, "pcol", None, None, "prow", None),
            P(),
        ),
        out_specs=(
            P(None, None, "prow", None, None, "pcol", None),
            P(None, None, "pcol", None, None, "prow", None),
        ),
        check_vma=False,
    )
```

```python
import functools

import jax
import jax.numpy as jnp
from jax import lax
from jax.experimental import pallas as pl
from jax.experimental.pallas import tpu as pltpu
from jax.sharding import PartitionSpec as P

OWN, NEAR = 0, 1
RIGHT, LEFT = 0, 1


def kernel(
    row_devices, col_devices, rows_loc, blk, cols_loc, diag_cols,
    s_in, u_in, d_in,
    o_all, d_out,
    u_buf, s_buf, o_mine, o_stage, acc,
    ring_send, ring_recv, sib_send, sib_recv, s_send, s_recv, near_send, near_recv,
    o_send, o_recv, mine_send, mine_recv, own_sem, keep_sem,
):
    nodes = s_in.shape[0]
    rows = rows_loc * blk
    chips = row_devices // 2
    half = chips // 2
    last = col_devices - 1
    p = lax.axis_index("prow")
    q = lax.axis_index("pcol")
    core = lax.rem(p, 2)
    flip = 1 - 2 * core
    inner = (q >= 1) & (q <= last - 1)
    helper = (q == 1) | (q == last - 1)
    end = (q == 0) | (q == last)
    near_q = jnp.where(q <= 1, 0, last)

    def along(n):
        high = n // half
        return n + high * (3 * half - 1 - 2 * n)

    chip = p // 2
    pos = along(chip)

    def slot(off):
        return along(lax.rem(pos + off + chips, chips)) * 2 + core

    def remote(src, dst, send, recv, to_p, to_q):
        return pltpu.make_async_remote_copy(
            src_ref=src, dst_ref=dst, send_sem=send, recv_sem=recv,
            device_id=(to_p, to_q), device_id_type=pl.DeviceIdType.MESH,
        )

    barrier = pltpu.get_barrier_semaphore()
    for step in range(1, row_devices):
        pl.semaphore_signal(
            barrier, inc=1, device_id=(lax.rem(p + step, row_devices), q),
            device_id_type=pl.DeviceIdType.MESH,
        )

    @pl.when(q > 0)
    def _():
        pl.semaphore_signal(
            barrier, inc=1, device_id=(p, q - 1), device_id_type=pl.DeviceIdType.MESH
        )

    @pl.when(q < last)
    def _():
        pl.semaphore_signal(
            barrier, inc=1, device_id=(p, q + 1), device_id_type=pl.DeviceIdType.MESH
        )

    @pl.when(inner)
    def _():
        pl.semaphore_wait(barrier, row_devices + 1)

    @pl.when(end)
    def _():
        pl.semaphore_wait(barrier, row_devices)

    def part(which, sn, at, step, way):
        if step < half:
            return u_buf.at[which, sn, at]
        cut = rows // 2
        return u_buf.at[which, sn, at, pl.ds(0 if way == RIGHT else cut, cut)]

    def ring(which, sn, way, step):
        sign = 1 if way == RIGHT else -1
        at = slot(-sign * (step - 1))
        dst = part(which, sn, at, step, way)
        src = u_in.at[sn] if (which == OWN and step == 1 and half > 1) else dst
        return remote(
            src, dst, ring_send.at[which, sn, way, step - 1],
            ring_recv.at[which, sn, way, step - 1], slot(sign), q,
        )

    def ring_wait(which, sn, way, step):
        sign = 1 if way == RIGHT else -1
        here = part(which, sn, slot(-sign * step), step, way)
        remote(
            here, here, ring_send.at[which, sn, way, step - 1],
            ring_recv.at[which, sn, way, step - 1], slot(sign), q,
        ).wait_recv()

    def sib(which, sn, off):
        at = slot(off)
        dst = u_buf.at[which, sn, at]
        src = u_in.at[sn] if (which == OWN and off == 0) else dst
        index = off + half - (which == OWN)
        return remote(
            src, dst, sib_send.at[which, sn, index], sib_recv.at[which, sn, index], p + flip, q
        )

    def offsets(which):
        return range(1 - half, half + 1) if which == OWN else range(-half, half)

    def sib_wait(which, sn, off):
        here = u_buf.at[which, sn, slot(off) + flip]
        index = off + half - (which == OWN)
        remote(
            here, here, sib_send.at[which, sn, index], sib_recv.at[which, sn, index], p + flip, q
        ).wait_recv()

    def ring_begin(which, sn):
        ring(which, sn, RIGHT, 1).start()
        ring(which, sn, LEFT, 1).start()
        sib(which, sn, 0).start()

    def ring_step(which, sn, step):
        for way in (RIGHT, LEFT):
            ring_wait(which, sn, way, step)
            if step < half:
                ring(which, sn, way, step + 1).start()
                sib(which, sn, -step if way == RIGHT else step).start()
        if step == half:
            sib(which, sn, half).start()

    def sib_all(which, sn):
        for off in offsets(which):
            sib_wait(which, sn, off)

    def ring_sent(which, sn):
        for step in range(1, half + (which == OWN)):
            for way in (RIGHT, LEFT):
                (ring if which == OWN else near_ring)(which, sn, way, step).wait_send()
        for off in offsets(which):
            sib(which, sn, off).wait_send()

    def near_ring(which, sn, way, step):
        at = slot(-step if way == RIGHT else step - 1)
        src = u_buf.at[which, sn, at]
        return remote(
            src, src, ring_send.at[which, sn, way, step - 1],
            ring_recv.at[which, sn, way, step - 1], slot(1 if way == RIGHT else -1), q,
        )

    def near_arrived(sn):
        for index in (0, 1):
            near(sn, index).wait_recv()
            if half > 1:
                near_ring(NEAR, sn, LEFT if index == 0 else RIGHT, 1).start()
            sib(NEAR, sn, -index).start()

    def near_steps(sn):
        for step in range(1, half):
            for way in (RIGHT, LEFT):
                off = -step - 1 if way == RIGHT else step
                here = u_buf.at[NEAR, sn, slot(off)]
                remote(
                    here, here, ring_send.at[NEAR, sn, way, step - 1],
                    ring_recv.at[NEAR, sn, way, step - 1], slot(1 if way == RIGHT else -1), q,
                ).wait_recv()
                if step + 1 < half:
                    near_ring(NEAR, sn, way, step + 1).start()
                sib(NEAR, sn, off).start()

    def s_copy(sn, at, way):
        src = s_buf.at[sn, at]
        return remote(
            src, src, s_send.at[sn, at, way], s_recv.at[sn, at], p,
            q + 1 if way == RIGHT else q - 1,
        )

    def s_own(sn, way):
        return remote(
            s_in.at[sn], s_buf.at[sn, q], s_send.at[sn, q, way], s_recv.at[sn, q], p,
            q + 1 if way == RIGHT else q - 1,
        )

    up_ok = q + 1 <= last - 1
    down_ok = q - 1 >= 1

    def s_begin(sn):
        @pl.when(up_ok)
        def _():
            s_own(sn, RIGHT).start()

        @pl.when(down_ok)
        def _():
            s_own(sn, LEFT).start()

    def s_sent(sn):
        @pl.when(up_ok)
        def _():
            s_own(sn, RIGHT).wait_send()

        @pl.when(down_ok)
        def _():
            s_own(sn, LEFT).wait_send()

        for dist in range(1, col_devices):
            @pl.when((q - dist >= 0) & inner & up_ok)
            def _():
                s_copy(sn, q - dist, RIGHT).wait_send()

            @pl.when((q + dist <= last) & inner & down_ok)
            def _():
                s_copy(sn, q + dist, LEFT).wait_send()

    def s_step(sn, dist):
        for way, at, there, onward in (
            (RIGHT, q - dist, q - dist >= 0, up_ok),
            (LEFT, q + dist, q + dist <= last, down_ok),
        ):
            @pl.when(there & inner)
            def _():
                s_copy(sn, at, way).wait_recv()

                @pl.when(onward)
                def _():
                    s_copy(sn, at, way).start()

    def near(sn, index):
        src = u_in.at[sn] if index == 0 else u_buf.at[OWN, sn, slot(-1)]
        return remote(
            src, u_buf.at[NEAR, sn, slot(-index)], near_send.at[sn, index],
            near_recv.at[sn, index], p,
            jnp.where(q == 0, 1, jnp.where(q == last, last - 1, near_q)),
        )

    def o_copy(sn, at, way, src=None):
        dst = o_all.at[sn, at]
        return remote(
            dst if src is None else src, dst, o_send.at[sn, at, way], o_recv.at[sn, at], p,
            q + 1 if way == RIGHT else q - 1,
        )

    def mine_each(sn, at, remote_do, local_do):
        for m in range(cols_loc):
            v = at + col_devices * m
            to_p = lax.rem(v, row_devices)
            k = v // row_devices
            if remote_do is not None:
                @pl.when(to_p != p)
                def _():
                    remote_do(
                        remote(
                            o_all.at[sn, at, m], o_mine.at[sn, k, p],
                            mine_send.at[sn, at, m], mine_recv.at[sn, k, p], to_p, q,
                        )
                    )

            if local_do is not None:
                @pl.when(to_p == p)
                def _():
                    local_do(
                        pltpu.make_async_copy(
                            o_all.at[sn, at, m], o_mine.at[sn, k, p], mine_recv.at[sn, k, p]
                        )
                    )

    def hand_out(sn, at):
        mine_each(sn, at, lambda c: c.start(), lambda c: c.start())

    def make_o(sn, which, at):
        sib_all(which, sn)
        acc[...] = jnp.zeros_like(acc)

        def add(src_p, carry):
            left = jnp.concatenate(
                [
                    s_buf[
                        sn, lax.rem(a * row_devices + src_p, col_devices),
                        (a * row_devices + src_p) // col_devices,
                    ]
                    for a in range(rows_loc)
                ],
                axis=1,
            )
            for m in range(cols_loc):
                acc[:rows, m * blk : (m + 1) * blk] += jnp.dot(
                    left, u_buf[which, sn, src_p, :, m * blk : (m + 1) * blk],
                    preferred_element_type=jnp.float32,
                )
            return carry

        lax.fori_loop(0, row_devices, add, 0)
        for m in range(cols_loc):
            o_stage[sn, which, m] = (-acc[:rows, m * blk : (m + 1) * blk]).astype(o_stage.dtype)
        stage = o_stage.at[sn, which]
        o_copy(sn, at, RIGHT, stage).start()
        o_copy(sn, at, LEFT, stage).start()
        keep = pltpu.make_async_copy(stage, o_all.at[sn, at], keep_sem.at[sn, which])
        keep.start()
        keep.wait()
        hand_out(sn, at)

    def o_step(sn, dist, extra):
        for way, origin, there, onward in (
            (RIGHT, q - dist, q - dist >= 1, q < last),
            (LEFT, q + dist, q + dist <= last - 1, q > 0),
        ):
            if extra:
                there = there & ((origin == 1) | (origin == last - 1))
                at = jnp.where(origin == 1, 0, last)
            else:
                at = origin
            @pl.when(there)
            def _():
                o_copy(sn, at, way).wait_recv()

                @pl.when(onward)
                def _():
                    o_copy(sn, at, way).start()

                hand_out(sn, at)

    def o_sent(sn):
        for extra in (False, True):
            if extra:
                first = helper
                at = near_q
            else:
                first = inner
                at = q
            @pl.when(first)
            def _():
                o_copy(sn, at, RIGHT).wait_send()
                o_copy(sn, at, LEFT).wait_send()
                mine_each(sn, at, lambda c: c.wait_send(), None)

            for dist in range(1, col_devices - 1):
                for way, origin, there, onward in (
                    (RIGHT, q - dist, q - dist >= 1, q < last),
                    (LEFT, q + dist, q + dist <= last - 1, q > 0),
                ):
                    if extra:
                        there = there & ((origin == 1) | (origin == last - 1))
                        at = jnp.where(origin == 1, 0, last)
                    else:
                        at = origin
                    @pl.when(there & onward)
                    def _():
                        o_copy(sn, at, way).wait_send()

                    @pl.when(there)
                    def _():
                        mine_each(sn, at, lambda c: c.wait_send(), None)

    def make_d(sn):
        acc[...] = jnp.zeros_like(acc)

        def add(src_p, carry):
            for k in range(diag_cols):
                pltpu.make_async_copy(
                    o_mine.at[sn, k, src_p], o_mine.at[sn, k, src_p], mine_recv.at[sn, k, src_p]
                ).wait()
                block = o_mine[sn, k, src_p]
                for m in range(cols_loc):
                    acc[k * blk : (k + 1) * blk, m * blk : (m + 1) * blk] += lax.dot_general(
                        block, u_buf[OWN, sn, src_p, :, m * blk : (m + 1) * blk],
                        (((0,), (0,)), ((), ())), preferred_element_type=jnp.float32,
                    )
            return carry

        lax.fori_loop(0, row_devices, add, 0)
        for k in range(diag_cols):
            for m in range(cols_loc):
                inner_sum = acc[k * blk : (k + 1) * blk, m * blk : (m + 1) * blk].T
                given = d_in[sn, m * blk : (m + 1) * blk, k * blk : (k + 1) * blk]
                d_out[sn, m * blk : (m + 1) * blk, k * blk : (k + 1) * blk] = (
                    given.astype(jnp.float32) - inner_sum
                ).astype(d_out.dtype)

    for sn in range(nodes):
        pltpu.make_async_copy(u_in.at[sn], u_buf.at[OWN, sn, p], own_sem.at[0, sn]).start()
        pltpu.make_async_copy(s_in.at[sn], s_buf.at[sn, q], own_sem.at[1, sn]).start()

    def near_begin(sn, index):
        @pl.when(end)
        def _():
            near(sn, index).start()

    def main_o(sn):
        @pl.when(inner)
        def _():
            make_o(sn, OWN, q)

        @pl.when(end)
        def _():
            sib_all(OWN, sn)

    def o_steps(sn, extra):
        for dist in range(1, col_devices - 1):
            o_step(sn, dist, extra)

    s_begin(0)
    near_begin(0, 0)
    ring_begin(OWN, 0)
    for sn in range(nodes):
        pltpu.make_async_copy(u_in.at[sn], u_buf.at[OWN, sn, p], own_sem.at[0, sn]).wait()
        pltpu.make_async_copy(s_in.at[sn], s_buf.at[sn, q], own_sem.at[1, sn]).wait()

    for sn in range(nodes):
        ring_step(OWN, sn, 1)
        near_begin(sn, 1)
        if sn + 1 < nodes:
            s_begin(sn + 1)
            near_begin(sn + 1, 0)
            ring_begin(OWN, sn + 1)
        if sn > 0:
            @pl.when(helper)
            def _():
                near_arrived(sn - 1)

        s_step(sn, 1)
        for step in range(2, half + 1):
            ring_step(OWN, sn, step)
        for dist in range(2, col_devices):
            s_step(sn, dist)
        main_o(sn)

    @pl.when(helper)
    def _():
        near_arrived(nodes - 1)

    for sn in range(nodes):
        o_steps(sn, False)

        @pl.when(helper)
        def _():
            near_steps(sn)
            make_o(sn, NEAR, near_q)

    for sn in range(nodes):
        o_steps(sn, True)

    for sn in range(nodes):
        make_d(sn)

    for sn in range(nodes):
        ring_sent(OWN, sn)
        s_sent(sn)
        o_sent(sn)

        @pl.when(helper)
        def _():
            ring_sent(NEAR, sn)

        @pl.when(end)
        def _():
            near(sn, 0).wait_send()
            near(sn, 1).wait_send()


def on_device(anc_inverse, factor_panel, diag_inverse, block_pattern):
    row_index = lax.axis_index("prow")
    col_index = lax.axis_index("pcol")
    row_devices = lax.axis_size("prow")
    col_devices = lax.axis_size("pcol")
    nodes, rows_loc, _, blk, cols_loc, _, _ = anc_inverse.shape
    panel_cols = factor_panel.shape[4]
    diag_cols = diag_inverse.shape[4]
    rows = rows_loc * blk
    pattern_grid = block_pattern.reshape(nodes, rows_loc, row_devices, cols_loc, col_devices)
    owned = lax.dynamic_slice_in_dim(pattern_grid, row_index, 1, 2)
    owned = lax.dynamic_slice_in_dim(owned, col_index, 1, 4)
    masked = jnp.where(owned[:, :, :, None, :, :, None] != 0, anc_inverse, jnp.zeros_like(anc_inverse))
    s_in = masked.reshape(nodes, rows, cols_loc, blk).transpose(0, 2, 1, 3)
    u_in = factor_panel.reshape(nodes, rows, panel_cols * blk)
    d_in = diag_inverse.reshape(nodes, panel_cols * blk, diag_cols * blk)
    half = row_devices // 4
    dma = pltpu.SemaphoreType.DMA
    bf16 = jnp.bfloat16
    o_all, d_out = pl.pallas_call(
        functools.partial(
            kernel, row_devices, col_devices, rows_loc, blk, panel_cols, diag_cols
        ),
        out_shape=(
            jax.ShapeDtypeStruct((nodes, col_devices, panel_cols, rows, blk), bf16),
            jax.ShapeDtypeStruct(d_in.shape, bf16),
        ),
        in_specs=[
            pl.BlockSpec(memory_space=pl.ANY),
            pl.BlockSpec(memory_space=pl.ANY),
            pl.BlockSpec(memory_space=pltpu.VMEM),
        ],
        out_specs=(
            pl.BlockSpec(memory_space=pl.ANY),
            pl.BlockSpec(memory_space=pltpu.VMEM),
        ),
        scratch_shapes=[
            pltpu.VMEM((2, nodes, row_devices, rows, panel_cols * blk), bf16),
            pltpu.VMEM((nodes, col_devices, cols_loc, rows, blk), bf16),
            pltpu.VMEM((nodes, diag_cols, row_devices, rows, blk), bf16),
            pltpu.VMEM((nodes, 2, panel_cols, rows, blk), bf16),
            pltpu.VMEM((max(rows, diag_cols * blk), panel_cols * blk), jnp.float32),
            dma((2, nodes, 2, half)),
            dma((2, nodes, 2, half)),
            dma((2, nodes, 2 * half)),
            dma((2, nodes, 2 * half)),
            dma((nodes, col_devices, 2)),
            dma((nodes, col_devices)),
            dma((nodes, 2)),
            dma((nodes, 2)),
            dma((nodes, col_devices, 2)),
            dma((nodes, col_devices)),
            dma((nodes, col_devices, panel_cols)),
            dma((nodes, diag_cols, row_devices)),
            dma((2, nodes)),
            dma((nodes, 2)),
        ],
        compiler_params=pltpu.CompilerParams(
            collective_id=0, has_side_effects=True, vmem_limit_bytes=62 * 1024 * 1024
        ),
        cost_estimate=pl.CostEstimate(
            flops=18 * 10**9, bytes_accessed=40 * 2**20, transcendentals=0
        ),
    )(s_in, u_in, d_in)
    off = lax.dynamic_slice_in_dim(o_all, col_index, 1, 1)[:, 0]
    sigma_off = off.transpose(0, 2, 1, 3).reshape(factor_panel.shape)
    return (sigma_off, d_out.reshape(diag_inverse.shape))


def solution(mesh):
    return jax.shard_map(
        on_device,
        mesh=mesh,
        in_specs=(
            P(None, None, "prow", None, None, "pcol", None),
            P(None, None, "prow", None, None, "pcol", None),
            P(None, None, "pcol", None, None, "prow", None),
            P(),
        ),
        out_specs=(
            P(None, None, "prow", None, None, "pcol", None),
            P(None, None, "pcol", None, None, "prow", None),
        ),
        check_vma=False,
    )
```

```python
import functools

import jax
import jax.numpy as jnp
from jax import lax
from jax.experimental import pallas as pl
from jax.experimental.pallas import tpu as pltpu
from jax.sharding import PartitionSpec as P

OWN, NEAR = 0, 1
RIGHT, LEFT = 0, 1


def kernel(
    row_devices, col_devices, rows_loc, blk, cols_loc, diag_cols,
    s_in, u_in, d_in,
    o_all, d_out,
    u_buf, s_buf, o_mine, o_stage, acc,
    ring_send, ring_recv, sib_send, sib_recv, s_send, s_recv, near_send, near_recv,
    o_send, o_recv, mine_send, mine_recv, own_sem, keep_sem,
):
    nodes = s_in.shape[0]
    rows = rows_loc * blk
    chips = row_devices // 2
    group = 4 if row_devices % 4 == 0 else 1
    half = chips // 2
    last = col_devices - 1
    p = lax.axis_index("prow")
    q = lax.axis_index("pcol")
    core = lax.rem(p, 2)
    flip = 1 - 2 * core
    inner = (q >= 1) & (q <= last - 1)
    helper = (q == 1) | (q == last - 1)
    end = (q == 0) | (q == last)
    near_q = jnp.where(q <= 1, 0, last)

    def along(n):
        high = n // half
        return n + high * (3 * half - 1 - 2 * n)

    chip = p // 2
    pos = along(chip)

    def panel(which, sn):
        return sn if which == OWN else nodes

    def slot(off):
        return along(lax.rem(pos + off + chips, chips)) * 2 + core

    def remote(src, dst, send, recv, to_p, to_q):
        return pltpu.make_async_remote_copy(
            src_ref=src, dst_ref=dst, send_sem=send, recv_sem=recv,
            device_id=(to_p, to_q), device_id_type=pl.DeviceIdType.MESH,
        )

    barrier = pltpu.get_barrier_semaphore()
    for step in range(1, row_devices):
        pl.semaphore_signal(
            barrier, inc=1, device_id=(lax.rem(p + step, row_devices), q),
            device_id_type=pl.DeviceIdType.MESH,
        )

    @pl.when(q > 0)
    def _():
        pl.semaphore_signal(
            barrier, inc=1, device_id=(p, q - 1), device_id_type=pl.DeviceIdType.MESH
        )

    @pl.when(q < last)
    def _():
        pl.semaphore_signal(
            barrier, inc=1, device_id=(p, q + 1), device_id_type=pl.DeviceIdType.MESH
        )

    @pl.when(inner)
    def _():
        pl.semaphore_wait(barrier, row_devices + 1)

    @pl.when(end)
    def _():
        pl.semaphore_wait(barrier, row_devices)

    def part(which, sn, at, step, way):
        if step < half:
            return u_buf.at[panel(which, sn), at]
        cut = rows // 2
        return u_buf.at[panel(which, sn), at, pl.ds(0 if way == RIGHT else cut, cut)]

    def ring(which, sn, way, step):
        sign = 1 if way == RIGHT else -1
        at = slot(-sign * (step - 1))
        dst = part(which, sn, at, step, way)
        src = u_in.at[sn] if (which == OWN and step == 1 and half > 1) else dst
        return remote(
            src, dst, ring_send.at[which, sn, way, step - 1],
            ring_recv.at[which, sn, way, step - 1], slot(sign), q,
        )

    def ring_wait(which, sn, way, step):
        sign = 1 if way == RIGHT else -1
        here = part(which, sn, slot(-sign * step), step, way)
        remote(
            here, here, ring_send.at[which, sn, way, step - 1],
            ring_recv.at[which, sn, way, step - 1], slot(sign), q,
        ).wait_recv()

    def sib(which, sn, off):
        at = slot(off)
        dst = u_buf.at[panel(which, sn), at]
        src = u_in.at[sn] if (which == OWN and off == 0) else dst
        index = off + half - (which == OWN)
        return remote(
            src, dst, sib_send.at[which, sn, index], sib_recv.at[which, sn, index], p + flip, q
        )

    def offsets(which):
        return range(1 - half, half + 1) if which == OWN else range(-half, half)

    def sib_wait(which, sn, off):
        here = u_buf.at[panel(which, sn), slot(off) + flip]
        index = off + half - (which == OWN)
        remote(
            here, here, sib_send.at[which, sn, index], sib_recv.at[which, sn, index], p + flip, q
        ).wait_recv()

    def ring_begin(which, sn):
        ring(which, sn, RIGHT, 1).start()
        ring(which, sn, LEFT, 1).start()
        sib(which, sn, 0).start()

    def ring_step(which, sn, step):
        for way in (RIGHT, LEFT):
            ring_wait(which, sn, way, step)
            if step < half:
                ring(which, sn, way, step + 1).start()
                sib(which, sn, -step if way == RIGHT else step).start()
        if step == half:
            sib(which, sn, half).start()

    def sib_all(which, sn):
        for off in offsets(which):
            sib_wait(which, sn, off)

    def ring_sent(which, sn):
        for step in range(1, half + (which == OWN)):
            for way in (RIGHT, LEFT):
                (ring if which == OWN else near_ring)(which, sn, way, step).wait_send()
        for off in offsets(which):
            sib(which, sn, off).wait_send()

    def near_ring(which, sn, way, step):
        at = slot(-step if way == RIGHT else step - 1)
        src = u_buf.at[panel(which, sn), at]
        return remote(
            src, src, ring_send.at[which, sn, way, step - 1],
            ring_recv.at[which, sn, way, step - 1], slot(1 if way == RIGHT else -1), q,
        )

    def near_arrived(sn):
        for index in (0, 1):
            near(sn, index).wait_recv()
            if half > 1:
                near_ring(NEAR, sn, LEFT if index == 0 else RIGHT, 1).start()
            sib(NEAR, sn, -index).start()

    def near_steps(sn):
        for step in range(1, half):
            for way in (RIGHT, LEFT):
                off = -step - 1 if way == RIGHT else step
                here = u_buf.at[panel(NEAR, sn), slot(off)]
                remote(
                    here, here, ring_send.at[NEAR, sn, way, step - 1],
                    ring_recv.at[NEAR, sn, way, step - 1], slot(1 if way == RIGHT else -1), q,
                ).wait_recv()
                if step + 1 < half:
                    near_ring(NEAR, sn, way, step + 1).start()
                sib(NEAR, sn, off).start()

    def s_copy(sn, at, way):
        src = s_buf.at[sn, at]
        return remote(
            src, src, s_send.at[sn, at, way], s_recv.at[sn, at], p,
            q + 1 if way == RIGHT else q - 1,
        )

    def s_own(sn, way):
        return remote(
            s_in.at[sn], s_buf.at[sn, q], s_send.at[sn, q, way], s_recv.at[sn, q], p,
            q + 1 if way == RIGHT else q - 1,
        )

    def lent(sn):
        return sn == 0

    def span(sn):
        return (1, last - 1) if lent(sn) else (0, last)

    def s_up(sn):
        return q + 1 <= span(sn)[1]

    def s_down(sn):
        return q - 1 >= span(sn)[0]

    def s_here(sn):
        return (q >= span(sn)[0]) & (q <= span(sn)[1])

    def s_begin(sn):
        @pl.when(s_up(sn))
        def _():
            s_own(sn, RIGHT).start()

        @pl.when(s_down(sn))
        def _():
            s_own(sn, LEFT).start()

    def s_sent(sn):
        @pl.when(s_up(sn))
        def _():
            s_own(sn, RIGHT).wait_send()

        @pl.when(s_down(sn))
        def _():
            s_own(sn, LEFT).wait_send()

        for dist in range(1, col_devices):
            @pl.when((q - dist >= 0) & s_here(sn) & s_up(sn))
            def _():
                s_copy(sn, q - dist, RIGHT).wait_send()

            @pl.when((q + dist <= last) & s_here(sn) & s_down(sn))
            def _():
                s_copy(sn, q + dist, LEFT).wait_send()

    def s_step(sn, dist):
        for way, at, there, onward in (
            (RIGHT, q - dist, q - dist >= 0, s_up(sn)),
            (LEFT, q + dist, q + dist <= last, s_down(sn)),
        ):
            @pl.when(there & s_here(sn))
            def _():
                s_copy(sn, at, way).wait_recv()

                @pl.when(onward)
                def _():
                    s_copy(sn, at, way).start()

    def near(sn, index):
        src = u_in.at[sn] if index == 0 else u_buf.at[panel(OWN, sn), slot(-1)]
        return remote(
            src, u_buf.at[panel(NEAR, sn), slot(-index)], near_send.at[sn, index],
            near_recv.at[sn, index], p,
            jnp.where(q == 0, 1, jnp.where(q == last, last - 1, near_q)),
        )

    def o_copy(sn, at, way, src=None):
        dst = o_all.at[sn, at]
        return remote(
            dst if src is None else src, dst, o_send.at[sn, at, way], o_recv.at[sn, at], p,
            q + 1 if way == RIGHT else q - 1,
        )

    def mine_each(sn, at, remote_do, local_do):
        for m in range(cols_loc):
            v = at + col_devices * m
            to_p = lax.rem(v, row_devices)
            k = v // row_devices
            if remote_do is not None:
                @pl.when(to_p != p)
                def _():
                    remote_do(
                        remote(
                            o_all.at[sn, at, m], o_mine.at[sn, k, p],
                            mine_send.at[sn, at, m], mine_recv.at[sn, k, p], to_p, q,
                        )
                    )

            if local_do is not None:
                @pl.when(to_p == p)
                def _():
                    local_do(
                        pltpu.make_async_copy(
                            o_all.at[sn, at, m], o_mine.at[sn, k, p], mine_recv.at[sn, k, p]
                        )
                    )

    def hand_out(sn, at):
        mine_each(sn, at, lambda c: c.start(), lambda c: c.start())

    def make_o(sn, which, at):
        sib_all(which, sn)
        acc[...] = jnp.zeros_like(acc)

        def add(step, carry):
            first = step * group
            left = jnp.concatenate(
                [
                    s_buf[
                        sn, lax.rem(a * row_devices + first + i, col_devices),
                        (a * row_devices + first + i) // col_devices,
                    ]
                    for i in range(group)
                    for a in range(rows_loc)
                ],
                axis=1,
            )
            for m in range(cols_loc):
                right = u_buf[
                    panel(which, sn), pl.ds(first, group), :, m * blk : (m + 1) * blk
                ].reshape(group * rows, blk)
                acc[:rows, m * blk : (m + 1) * blk] += jnp.dot(
                    left, right, preferred_element_type=jnp.float32
                )
            return carry

        lax.fori_loop(0, row_devices // group, add, 0)
        for m in range(cols_loc):
            o_stage[sn, which, m] = (-acc[:rows, m * blk : (m + 1) * blk]).astype(o_stage.dtype)
        stage = o_stage.at[sn, which]
        @pl.when(q < last)
        def _():
            o_copy(sn, at, RIGHT, stage).start()

        @pl.when(q > 0)
        def _():
            o_copy(sn, at, LEFT, stage).start()

        keep = pltpu.make_async_copy(stage, o_all.at[sn, at], keep_sem.at[sn, which])
        keep.start()
        keep.wait()
        hand_out(sn, at)

    def o_step(sn, dist, extra):
        for way, origin, there, onward in (
            (RIGHT, q - dist, q - dist >= span(sn)[0], q < last),
            (LEFT, q + dist, q + dist <= span(sn)[1], q > 0),
        ):
            if extra:
                there = there & ((origin == 1) | (origin == last - 1))
                at = jnp.where(origin == 1, 0, last)
            else:
                at = origin
            @pl.when(there)
            def _():
                o_copy(sn, at, way).wait_recv()

                @pl.when(onward)
                def _():
                    o_copy(sn, at, way).start()

                hand_out(sn, at)

    def o_sent(sn):
        for extra in (False, True) if lent(sn) else (False,):
            if extra:
                first = helper
                at = near_q
            else:
                first = s_here(sn)
                at = q

            @pl.when(first & (q < last))
            def _():
                o_copy(sn, at, RIGHT).wait_send()

            @pl.when(first & (q > 0))
            def _():
                o_copy(sn, at, LEFT).wait_send()

            @pl.when(first)
            def _():
                mine_each(sn, at, lambda c: c.wait_send(), None)

            for dist in range(1, span(sn)[1] + 1):
                for way, origin, there, onward in (
                    (RIGHT, q - dist, q - dist >= span(sn)[0], q < last),
                    (LEFT, q + dist, q + dist <= span(sn)[1], q > 0),
                ):
                    if extra:
                        there = there & ((origin == 1) | (origin == last - 1))
                        at = jnp.where(origin == 1, 0, last)
                    else:
                        at = origin
                    @pl.when(there & onward)
                    def _():
                        o_copy(sn, at, way).wait_send()

                    @pl.when(there)
                    def _():
                        mine_each(sn, at, lambda c: c.wait_send(), None)

    def make_d(sn):
        acc[...] = jnp.zeros_like(acc)

        def add(step, carry):
            first = step * group
            for k in range(diag_cols):
                for i in range(group):
                    here = o_mine.at[sn, k, first + i]
                    pltpu.make_async_copy(here, here, mine_recv.at[sn, k, first + i]).wait()
                block = o_mine[sn, k, pl.ds(first, group)].reshape(group * rows, blk)
                for m in range(cols_loc):
                    right = u_buf[
                        panel(OWN, sn), pl.ds(first, group), :, m * blk : (m + 1) * blk
                    ].reshape(group * rows, blk)
                    acc[k * blk : (k + 1) * blk, m * blk : (m + 1) * blk] += lax.dot_general(
                        block, right, (((0,), (0,)), ((), ())),
                        preferred_element_type=jnp.float32,
                    )
            return carry

        lax.fori_loop(0, row_devices // group, add, 0)
        for k in range(diag_cols):
            for m in range(cols_loc):
                inner_sum = acc[k * blk : (k + 1) * blk, m * blk : (m + 1) * blk].T
                given = d_in[sn, m * blk : (m + 1) * blk, k * blk : (k + 1) * blk]
                d_out[sn, m * blk : (m + 1) * blk, k * blk : (k + 1) * blk] = (
                    given.astype(jnp.float32) - inner_sum
                ).astype(d_out.dtype)

    for sn in range(nodes):
        pltpu.make_async_copy(u_in.at[sn], u_buf.at[panel(OWN, sn), p], own_sem.at[0, sn]).start()
        pltpu.make_async_copy(s_in.at[sn], s_buf.at[sn, q], own_sem.at[1, sn]).start()

    def near_begin(sn, index):
        if lent(sn):
            @pl.when(end)
            def _():
                near(sn, index).start()

    def main_o(sn):
        @pl.when(s_here(sn))
        def _():
            make_o(sn, OWN, q)

        @pl.when(jnp.logical_not(s_here(sn)))
        def _():
            sib_all(OWN, sn)

    def lent_o(sn):
        if lent(sn):
            @pl.when(helper)
            def _():
                near_steps(sn)
                make_o(sn, NEAR, near_q)

    for sn in range(nodes):
        near_begin(sn, 0)
        s_begin(sn)
    ring_begin(OWN, 0)
    for sn in range(nodes):
        pltpu.make_async_copy(u_in.at[sn], u_buf.at[panel(OWN, sn), p], own_sem.at[0, sn]).wait()
        pltpu.make_async_copy(s_in.at[sn], s_buf.at[sn, q], own_sem.at[1, sn]).wait()

    for sn in range(nodes):
        ring_step(OWN, sn, 1)
        near_begin(sn, 1)
        if sn + 1 < nodes:
            ring_begin(OWN, sn + 1)
        if sn == 0:
            for other in range(nodes):
                s_step(other, 1)
        for step in range(2, half + 1):
            ring_step(OWN, sn, step)
        if sn == 0:
            for dist in range(2, col_devices - 1):
                for other in range(nodes):
                    s_step(other, dist)
        s_step(sn, col_devices - 1)
        main_o(sn)
        if lent(sn):
            @pl.when(helper)
            def _():
                near_arrived(sn)

    for dist in range(1, col_devices):
        o_step(0, dist, False)
    lent_o(0)
    for dist in range(1, col_devices):
        for sn in range(1, nodes):
            o_step(sn, dist, False)
        o_step(0, dist, True)

    for sn in range(nodes):
        make_d(sn)

    for sn in range(nodes):
        ring_sent(OWN, sn)
        s_sent(sn)
        o_sent(sn)

        if lent(sn):
            @pl.when(helper)
            def _():
                ring_sent(NEAR, sn)

            @pl.when(end)
            def _():
                near(sn, 0).wait_send()
                near(sn, 1).wait_send()


def on_device(anc_inverse, factor_panel, diag_inverse, block_pattern):
    row_index = lax.axis_index("prow")
    col_index = lax.axis_index("pcol")
    row_devices = lax.axis_size("prow")
    col_devices = lax.axis_size("pcol")
    nodes, rows_loc, _, blk, cols_loc, _, _ = anc_inverse.shape
    panel_cols = factor_panel.shape[4]
    diag_cols = diag_inverse.shape[4]
    rows = rows_loc * blk
    pattern_grid = block_pattern.reshape(nodes, rows_loc, row_devices, cols_loc, col_devices)
    owned = lax.dynamic_slice_in_dim(pattern_grid, row_index, 1, 2)
    owned = lax.dynamic_slice_in_dim(owned, col_index, 1, 4)
    masked = jnp.where(owned[:, :, :, None, :, :, None] != 0, anc_inverse, jnp.zeros_like(anc_inverse))
    s_in = masked.reshape(nodes, rows, cols_loc, blk).transpose(0, 2, 1, 3)
    u_in = factor_panel.reshape(nodes, rows, panel_cols * blk)
    d_in = diag_inverse.reshape(nodes, panel_cols * blk, diag_cols * blk)
    half = row_devices // 4
    dma = pltpu.SemaphoreType.DMA
    bf16 = jnp.bfloat16
    o_all, d_out = pl.pallas_call(
        functools.partial(
            kernel, row_devices, col_devices, rows_loc, blk, panel_cols, diag_cols
        ),
        out_shape=(
            jax.ShapeDtypeStruct((nodes, col_devices, panel_cols, rows, blk), bf16),
            jax.ShapeDtypeStruct(d_in.shape, bf16),
        ),
        in_specs=[
            pl.BlockSpec(memory_space=pl.ANY),
            pl.BlockSpec(memory_space=pl.ANY),
            pl.BlockSpec(memory_space=pltpu.VMEM),
        ],
        out_specs=(
            pl.BlockSpec(memory_space=pl.ANY),
            pl.BlockSpec(memory_space=pltpu.VMEM),
        ),
        scratch_shapes=[
            pltpu.VMEM((nodes + 1, row_devices, rows, panel_cols * blk), bf16),
            pltpu.VMEM((nodes, col_devices, cols_loc, rows, blk), bf16),
            pltpu.VMEM((nodes, diag_cols, row_devices, rows, blk), bf16),
            pltpu.VMEM((nodes, 2, panel_cols, rows, blk), bf16),
            pltpu.VMEM((max(rows, diag_cols * blk), panel_cols * blk), jnp.float32),
            dma((2, nodes, 2, half)),
            dma((2, nodes, 2, half)),
            dma((2, nodes, 2 * half)),
            dma((2, nodes, 2 * half)),
            dma((nodes, col_devices, 2)),
            dma((nodes, col_devices)),
            dma((nodes, 2)),
            dma((nodes, 2)),
            dma((nodes, col_devices, 2)),
            dma((nodes, col_devices)),
            dma((nodes, col_devices, panel_cols)),
            dma((nodes, diag_cols, row_devices)),
            dma((2, nodes)),
            dma((nodes, 2)),
        ],
        compiler_params=pltpu.CompilerParams(
            collective_id=0, has_side_effects=True, vmem_limit_bytes=62 * 1024 * 1024
        ),
        cost_estimate=pl.CostEstimate(
            flops=18 * 10**9, bytes_accessed=40 * 2**20, transcendentals=0
        ),
    )(s_in, u_in, d_in)
    off = lax.dynamic_slice_in_dim(o_all, col_index, 1, 1)[:, 0]
    sigma_off = off.transpose(0, 2, 1, 3).reshape(factor_panel.shape)
    return (sigma_off, d_out.reshape(diag_inverse.shape))


def solution(mesh):
    return jax.shard_map(
        on_device,
        mesh=mesh,
        in_specs=(
            P(None, None, "prow", None, None, "pcol", None),
            P(None, None, "prow", None, None, "pcol", None),
            P(None, None, "pcol", None, None, "prow", None),
            P(),
        ),
        out_specs=(
            P(None, None, "prow", None, None, "pcol", None),
            P(None, None, "pcol", None, None, "prow", None),
        ),
        check_vma=False,
    )
```

```python
import functools

import jax
import jax.numpy as jnp
from jax import lax
from jax.experimental import pallas as pl
from jax.experimental.pallas import tpu as pltpu
from jax.sharding import PartitionSpec as P

OWN, NEAR = 0, 1
RIGHT, LEFT = 0, 1


def kernel(
    row_devices, col_devices, rows_loc, blk, cols_loc, diag_cols,
    s_in, u_in, d_in,
    o_all, d_out,
    u_buf, s_buf, o_mine, o_stage, acc,
    ring_send, ring_recv, sib_send, sib_recv, s_send, s_recv, near_send, near_recv,
    o_send, o_recv, mine_send, mine_recv, own_sem, keep_sem,
):
    nodes = s_in.shape[0]
    rows = rows_loc * blk
    chips = row_devices // 2
    parts = 2 if cols_loc % 2 == 0 else 1
    wide = cols_loc // parts
    group = 4 if row_devices % 4 == 0 else 1
    half = chips // 2
    last = col_devices - 1
    p = lax.axis_index("prow")
    q = lax.axis_index("pcol")
    core = lax.rem(p, 2)
    flip = 1 - 2 * core
    inner = (q >= 1) & (q <= last - 1)
    helper = (q == 1) | (q == last - 1)
    end = (q == 0) | (q == last)
    near_q = jnp.where(q <= 1, 0, last)

    def along(n):
        high = n // half
        return n + high * (3 * half - 1 - 2 * n)

    chip = p // 2
    pos = along(chip)

    def panel(which, sn):
        return sn if which == OWN else nodes

    def slot(off):
        return along(lax.rem(pos + off + chips, chips)) * 2 + core

    def remote(src, dst, send, recv, to_p, to_q):
        return pltpu.make_async_remote_copy(
            src_ref=src, dst_ref=dst, send_sem=send, recv_sem=recv,
            device_id=(to_p, to_q), device_id_type=pl.DeviceIdType.MESH,
        )

    barrier = pltpu.get_barrier_semaphore()
    for step in range(1, row_devices):
        pl.semaphore_signal(
            barrier, inc=1, device_id=(lax.rem(p + step, row_devices), q),
            device_id_type=pl.DeviceIdType.MESH,
        )

    @pl.when(q > 0)
    def _():
        pl.semaphore_signal(
            barrier, inc=1, device_id=(p, q - 1), device_id_type=pl.DeviceIdType.MESH
        )

    @pl.when(q < last)
    def _():
        pl.semaphore_signal(
            barrier, inc=1, device_id=(p, q + 1), device_id_type=pl.DeviceIdType.MESH
        )

    @pl.when(inner)
    def _():
        pl.semaphore_wait(barrier, row_devices + 1)

    @pl.when(end)
    def _():
        pl.semaphore_wait(barrier, row_devices)

    def part(which, sn, at, step, way):
        if step < half:
            return u_buf.at[panel(which, sn), at]
        cut = rows // 2
        return u_buf.at[panel(which, sn), at, pl.ds(0 if way == RIGHT else cut, cut)]

    def ring(which, sn, way, step):
        sign = 1 if way == RIGHT else -1
        at = slot(-sign * (step - 1))
        dst = part(which, sn, at, step, way)
        src = u_in.at[sn] if (which == OWN and step == 1 and half > 1) else dst
        return remote(
            src, dst, ring_send.at[which, sn, way, step - 1],
            ring_recv.at[which, sn, way, step - 1], slot(sign), q,
        )

    def ring_wait(which, sn, way, step):
        sign = 1 if way == RIGHT else -1
        here = part(which, sn, slot(-sign * step), step, way)
        remote(
            here, here, ring_send.at[which, sn, way, step - 1],
            ring_recv.at[which, sn, way, step - 1], slot(sign), q,
        ).wait_recv()

    def sib(which, sn, off):
        at = slot(off)
        dst = u_buf.at[panel(which, sn), at]
        src = u_in.at[sn] if (which == OWN and off == 0) else dst
        index = off + half - (which == OWN)
        return remote(
            src, dst, sib_send.at[which, sn, index], sib_recv.at[which, sn, index], p + flip, q
        )

    def offsets(which):
        return range(1 - half, half + 1) if which == OWN else range(-half, half)

    def sib_wait(which, sn, off):
        here = u_buf.at[panel(which, sn), slot(off) + flip]
        index = off + half - (which == OWN)
        remote(
            here, here, sib_send.at[which, sn, index], sib_recv.at[which, sn, index], p + flip, q
        ).wait_recv()

    def ring_begin(which, sn):
        ring(which, sn, RIGHT, 1).start()
        ring(which, sn, LEFT, 1).start()
        sib(which, sn, 0).start()

    def ring_step(which, sn, step):
        for way in (RIGHT, LEFT):
            ring_wait(which, sn, way, step)
            if step < half:
                ring(which, sn, way, step + 1).start()
                sib(which, sn, -step if way == RIGHT else step).start()
        if step == half:
            sib(which, sn, half).start()

    def sib_all(which, sn):
        for off in offsets(which):
            sib_wait(which, sn, off)

    def ring_sent(which, sn):
        for step in range(1, half + (which == OWN)):
            for way in (RIGHT, LEFT):
                (ring if which == OWN else near_ring)(which, sn, way, step).wait_send()
        for off in offsets(which):
            sib(which, sn, off).wait_send()

    def near_ring(which, sn, way, step):
        at = slot(-step if way == RIGHT else step - 1)
        src = u_buf.at[panel(which, sn), at]
        return remote(
            src, src, ring_send.at[which, sn, way, step - 1],
            ring_recv.at[which, sn, way, step - 1], slot(1 if way == RIGHT else -1), q,
        )

    def near_arrived(sn):
        for index in (0, 1):
            near(sn, index).wait_recv()
            if half > 1:
                near_ring(NEAR, sn, LEFT if index == 0 else RIGHT, 1).start()
            sib(NEAR, sn, -index).start()

    def near_steps(sn):
        for step in range(1, half):
            for way in (RIGHT, LEFT):
                off = -step - 1 if way == RIGHT else step
                here = u_buf.at[panel(NEAR, sn), slot(off)]
                remote(
                    here, here, ring_send.at[NEAR, sn, way, step - 1],
                    ring_recv.at[NEAR, sn, way, step - 1], slot(1 if way == RIGHT else -1), q,
                ).wait_recv()
                if step + 1 < half:
                    near_ring(NEAR, sn, way, step + 1).start()
                sib(NEAR, sn, off).start()

    def s_copy(sn, at, way, h, own=False):
        dst = s_buf.at[sn, at, pl.ds(h * wide, wide)]
        return remote(
            s_in.at[sn, pl.ds(h * wide, wide)] if own else dst, dst,
            s_send.at[sn, at, way, h], s_recv.at[sn, at, h], p,
            q + 1 if way == RIGHT else q - 1,
        )

    def lent(sn):
        return sn == 0

    def span(sn):
        return (1, last - 1) if lent(sn) else (0, last)

    def s_up(sn):
        return q + 1 <= span(sn)[1]

    def s_down(sn):
        return q - 1 >= span(sn)[0]

    def s_here(sn):
        return (q >= span(sn)[0]) & (q <= span(sn)[1])

    def s_begin(sn):
        for h in range(parts):
            @pl.when(s_up(sn))
            def _():
                s_copy(sn, q, RIGHT, h, True).start()

            @pl.when(s_down(sn))
            def _():
                s_copy(sn, q, LEFT, h, True).start()

    def s_sent(sn):
        for h in range(parts):
            @pl.when(s_up(sn))
            def _():
                s_copy(sn, q, RIGHT, h, True).wait_send()

            @pl.when(s_down(sn))
            def _():
                s_copy(sn, q, LEFT, h, True).wait_send()

            for dist in range(1, col_devices):
                @pl.when((q - dist >= 0) & s_here(sn) & s_up(sn))
                def _():
                    s_copy(sn, q - dist, RIGHT, h).wait_send()

                @pl.when((q + dist <= last) & s_here(sn) & s_down(sn))
                def _():
                    s_copy(sn, q + dist, LEFT, h).wait_send()

    def s_step(sn, dist):
        for h in range(parts):
            for way, at, there, onward in (
                (RIGHT, q - dist, q - dist >= 0, s_up(sn)),
                (LEFT, q + dist, q + dist <= last, s_down(sn)),
            ):
                @pl.when(there & s_here(sn))
                def _():
                    s_copy(sn, at, way, h).wait_recv()

                    @pl.when(onward)
                    def _():
                        s_copy(sn, at, way, h).start()

    def near(sn, index):
        src = u_in.at[sn] if index == 0 else u_buf.at[panel(OWN, sn), slot(-1)]
        return remote(
            src, u_buf.at[panel(NEAR, sn), slot(-index)], near_send.at[sn, index],
            near_recv.at[sn, index], p,
            jnp.where(q == 0, 1, jnp.where(q == last, last - 1, near_q)),
        )

    def o_copy(sn, at, way, h, src=None):
        dst = o_all.at[sn, at, pl.ds(h * wide, wide)]
        return remote(
            dst if src is None else src, dst, o_send.at[sn, at, way, h],
            o_recv.at[sn, at, h], p, q + 1 if way == RIGHT else q - 1,
        )

    def mine_each(sn, at, h, remote_do, local_do):
        for m in range(h * wide, (h + 1) * wide):
            v = at + col_devices * m
            to_p = lax.rem(v, row_devices)
            k = v // row_devices

            @pl.when(to_p != p)
            def _():
                remote_do(
                    remote(
                        o_all.at[sn, at, m], o_mine.at[sn, k, p],
                        mine_send.at[sn, at, m], mine_recv.at[sn, k, p], to_p, q,
                    )
                )

            if local_do is not None:
                @pl.when(to_p == p)
                def _():
                    local_do(
                        pltpu.make_async_copy(
                            o_all.at[sn, at, m], o_mine.at[sn, k, p], mine_recv.at[sn, k, p]
                        )
                    )

    def hand_out(sn, at, h):
        mine_each(sn, at, h, lambda c: c.start(), lambda c: c.start())

    def make_o(sn, which, at):
        sib_all(which, sn)
        acc[...] = jnp.zeros_like(acc)
        for h in range(parts):
            make_part(sn, which, at, h)

    def make_part(sn, which, at, h):
        def add(step, carry):
            first = step * group
            left = jnp.concatenate(
                [
                    s_buf[
                        sn, lax.rem(a * row_devices + first + i, col_devices),
                        (a * row_devices + first + i) // col_devices,
                    ]
                    for i in range(group)
                    for a in range(rows_loc)
                ],
                axis=1,
            )
            for m in range(h * wide, (h + 1) * wide):
                right = u_buf[
                    panel(which, sn), pl.ds(first, group), :, m * blk : (m + 1) * blk
                ].reshape(group * rows, blk)
                acc[:rows, m * blk : (m + 1) * blk] += jnp.dot(
                    left, right, preferred_element_type=jnp.float32
                )
            return carry

        lax.fori_loop(0, row_devices // group, add, 0)
        for m in range(h * wide, (h + 1) * wide):
            o_stage[sn, which, m] = (-acc[:rows, m * blk : (m + 1) * blk]).astype(o_stage.dtype)
        stage = o_stage.at[sn, which, pl.ds(h * wide, wide)]

        @pl.when(q < last)
        def _():
            o_copy(sn, at, RIGHT, h, stage).start()

        @pl.when(q > 0)
        def _():
            o_copy(sn, at, LEFT, h, stage).start()

        keep = pltpu.make_async_copy(
            stage, o_all.at[sn, at, pl.ds(h * wide, wide)], keep_sem.at[sn, which, h]
        )
        keep.start()
        keep.wait()
        hand_out(sn, at, h)

    def o_ways(sn, dist, extra):
        for way, origin, there, onward in (
            (RIGHT, q - dist, q - dist >= span(sn)[0], q < last),
            (LEFT, q + dist, q + dist <= span(sn)[1], q > 0),
        ):
            if extra:
                there = there & ((origin == 1) | (origin == last - 1))
                yield way, jnp.where(origin == 1, 0, last), there, onward
            else:
                yield way, origin, there, onward

    def o_step(sn, dist, extra):
        for h in range(parts):
            for way, at, there, onward in o_ways(sn, dist, extra):
                @pl.when(there)
                def _():
                    o_copy(sn, at, way, h).wait_recv()

                    @pl.when(onward)
                    def _():
                        o_copy(sn, at, way, h).start()

                    hand_out(sn, at, h)

    def o_sent(sn):
        for h in range(parts):
            for extra in (False, True) if lent(sn) else (False,):
                first, made = (helper, near_q) if extra else (s_here(sn), q)

                @pl.when(first & (q < last))
                def _():
                    o_copy(sn, made, RIGHT, h).wait_send()

                @pl.when(first & (q > 0))
                def _():
                    o_copy(sn, made, LEFT, h).wait_send()

                @pl.when(first)
                def _():
                    mine_each(sn, made, h, lambda c: c.wait_send(), None)

                for dist in range(1, span(sn)[1] + 1):
                    for way, at, there, onward in o_ways(sn, dist, extra):
                        @pl.when(there & onward)
                        def _():
                            o_copy(sn, at, way, h).wait_send()

                        @pl.when(there)
                        def _():
                            mine_each(sn, at, h, lambda c: c.wait_send(), None)

    def make_d(sn):
        acc[...] = jnp.zeros_like(acc)

        def add(step, carry):
            first = step * group
            for k in range(diag_cols):
                for i in range(group):
                    here = o_mine.at[sn, k, first + i]
                    pltpu.make_async_copy(here, here, mine_recv.at[sn, k, first + i]).wait()
                block = o_mine[sn, k, pl.ds(first, group)].reshape(group * rows, blk).T
                for m in range(cols_loc):
                    right = u_buf[
                        panel(OWN, sn), pl.ds(first, group), :, m * blk : (m + 1) * blk
                    ].reshape(group * rows, blk)
                    acc[k * blk : (k + 1) * blk, m * blk : (m + 1) * blk] += jnp.dot(
                        block, right, preferred_element_type=jnp.float32
                    )
            return carry

        lax.fori_loop(0, row_devices // group, add, 0)
        for k in range(diag_cols):
            for m in range(cols_loc):
                inner_sum = acc[k * blk : (k + 1) * blk, m * blk : (m + 1) * blk].T
                given = d_in[sn, m * blk : (m + 1) * blk, k * blk : (k + 1) * blk]
                d_out[sn, m * blk : (m + 1) * blk, k * blk : (k + 1) * blk] = (
                    given.astype(jnp.float32) - inner_sum
                ).astype(d_out.dtype)

    for sn in range(nodes):
        pltpu.make_async_copy(u_in.at[sn], u_buf.at[panel(OWN, sn), p], own_sem.at[0, sn]).start()
        pltpu.make_async_copy(s_in.at[sn], s_buf.at[sn, q], own_sem.at[1, sn]).start()

    def near_begin(sn, index):
        if lent(sn):
            @pl.when(end)
            def _():
                near(sn, index).start()

    def main_o(sn):
        @pl.when(s_here(sn))
        def _():
            make_o(sn, OWN, q)

        @pl.when(jnp.logical_not(s_here(sn)))
        def _():
            sib_all(OWN, sn)

    def lent_o(sn):
        if lent(sn):
            @pl.when(helper)
            def _():
                near_steps(sn)
                make_o(sn, NEAR, near_q)

    for sn in range(nodes):
        s_begin(sn)
    ring_begin(OWN, 0)
    for sn in range(nodes):
        pltpu.make_async_copy(u_in.at[sn], u_buf.at[panel(OWN, sn), p], own_sem.at[0, sn]).wait()
        pltpu.make_async_copy(s_in.at[sn], s_buf.at[sn, q], own_sem.at[1, sn]).wait()

    for sn in range(nodes):
        ring_step(OWN, sn, 1)
        if sn + 1 < nodes:
            ring_begin(OWN, sn + 1)
        if sn == 0:
            for other in range(nodes):
                s_step(other, 1)
            near_begin(0, 0)
            near_begin(0, 1)
        for step in range(2, half + 1):
            ring_step(OWN, sn, step)
        if sn == 0:
            for dist in range(2, col_devices - 1):
                for other in range(nodes):
                    s_step(other, dist)
        s_step(sn, col_devices - 1)
        main_o(sn)
        if lent(sn):
            @pl.when(helper)
            def _():
                near_arrived(sn)

    for dist in range(1, col_devices):
        o_step(0, dist, False)
    lent_o(0)
    for dist in range(1, col_devices):
        o_step(0, dist, True)
        for sn in range(1, nodes):
            o_step(sn, dist, False)

    for sn in range(nodes):
        make_d(sn)

    for sn in range(nodes):
        ring_sent(OWN, sn)
        s_sent(sn)
        o_sent(sn)

        if lent(sn):
            @pl.when(helper)
            def _():
                ring_sent(NEAR, sn)

            @pl.when(end)
            def _():
                near(sn, 0).wait_send()
                near(sn, 1).wait_send()


def on_device(anc_inverse, factor_panel, diag_inverse, block_pattern):
    row_index = lax.axis_index("prow")
    col_index = lax.axis_index("pcol")
    row_devices = lax.axis_size("prow")
    col_devices = lax.axis_size("pcol")
    nodes, rows_loc, _, blk, cols_loc, _, _ = anc_inverse.shape
    panel_cols = factor_panel.shape[4]
    diag_cols = diag_inverse.shape[4]
    rows = rows_loc * blk
    pattern_grid = block_pattern.reshape(nodes, rows_loc, row_devices, cols_loc, col_devices)
    owned = lax.dynamic_slice_in_dim(pattern_grid, row_index, 1, 2)
    owned = lax.dynamic_slice_in_dim(owned, col_index, 1, 4)
    masked = jnp.where(owned[:, :, :, None, :, :, None] != 0, anc_inverse, jnp.zeros_like(anc_inverse))
    s_in = masked.reshape(nodes, rows, cols_loc, blk).transpose(0, 2, 1, 3)
    u_in = factor_panel.reshape(nodes, rows, panel_cols * blk)
    d_in = diag_inverse.reshape(nodes, panel_cols * blk, diag_cols * blk)
    half = row_devices // 4
    parts = 2 if panel_cols % 2 == 0 else 1
    dma = pltpu.SemaphoreType.DMA
    bf16 = jnp.bfloat16
    o_all, d_out = pl.pallas_call(
        functools.partial(
            kernel, row_devices, col_devices, rows_loc, blk, panel_cols, diag_cols
        ),
        out_shape=(
            jax.ShapeDtypeStruct((nodes, col_devices, panel_cols, rows, blk), bf16),
            jax.ShapeDtypeStruct(d_in.shape, bf16),
        ),
        in_specs=[
            pl.BlockSpec(memory_space=pl.ANY),
            pl.BlockSpec(memory_space=pl.ANY),
            pl.BlockSpec(memory_space=pltpu.VMEM),
        ],
        out_specs=(
            pl.BlockSpec(memory_space=pl.ANY),
            pl.BlockSpec(memory_space=pltpu.VMEM),
        ),
        scratch_shapes=[
            pltpu.VMEM((nodes + 1, row_devices, rows, panel_cols * blk), bf16),
            pltpu.VMEM((nodes, col_devices, cols_loc, rows, blk), bf16),
            pltpu.VMEM((nodes, diag_cols, row_devices, rows, blk), bf16),
            pltpu.VMEM((nodes, 2, panel_cols, rows, blk), bf16),
            pltpu.VMEM((max(rows, diag_cols * blk), panel_cols * blk), jnp.float32),
            dma((2, nodes, 2, half)),
            dma((2, nodes, 2, half)),
            dma((2, nodes, 2 * half)),
            dma((2, nodes, 2 * half)),
            dma((nodes, col_devices, 2, parts)),
            dma((nodes, col_devices, parts)),
            dma((nodes, 2)),
            dma((nodes, 2)),
            dma((nodes, col_devices, 2, parts)),
            dma((nodes, col_devices, parts)),
            dma((nodes, col_devices, panel_cols)),
            dma((nodes, diag_cols, row_devices)),
            dma((2, nodes)),
            dma((nodes, 2, parts)),
        ],
        compiler_params=pltpu.CompilerParams(
            collective_id=0, has_side_effects=True, vmem_limit_bytes=62 * 1024 * 1024
        ),
        cost_estimate=pl.CostEstimate(
            flops=18 * 10**9, bytes_accessed=40 * 2**20, transcendentals=0
        ),
    )(s_in, u_in, d_in)
    off = lax.dynamic_slice_in_dim(o_all, col_index, 1, 1)[:, 0]
    sigma_off = off.transpose(0, 2, 1, 3).reshape(factor_panel.shape)
    return (sigma_off, d_out.reshape(diag_inverse.shape))


def solution(mesh):
    return jax.shard_map(
        on_device,
        mesh=mesh,
        in_specs=(
            P(None, None, "prow", None, None, "pcol", None),
            P(None, None, "prow", None, None, "pcol", None),
            P(None, None, "pcol", None, None, "prow", None),
            P(),
        ),
        out_specs=(
            P(None, None, "prow", None, None, "pcol", None),
            P(None, None, "pcol", None, None, "prow", None),
        ),
        check_vma=False,
    )
```
